512 devices in a mesh: ht: 16 (over z_lo, core), wt: 32 (over x, y, z_hi).
Axes of the slice: x: 4, y: 4, z: 16 (z_hi: 2, z_lo: 8; z = z_hi * 8 + z_lo), core: 2. Of those that a mesh axis runs over, the one named last changes fastest.
Arguments:
- queries: bfloat16 [256, 256, 1024], P('ht', 'wt'), may hold values from -30 to 30
- keys_new: bfloat16 [256, 256, 1024], P('ht', 'wt'), may hold values from -10 to 10, as said below
- values_new: bfloat16 [256, 256, 1024], P('ht', 'wt'), may hold values from -6 to 6
- keys_cache: bfloat16 [1, 256, 256, 1024], P(None, 'ht', 'wt'), may hold values from -10 to 10, as said below
- values_cache: bfloat16 [1, 256, 256, 1024], P(None, 'ht', 'wt'), may hold values from -6 to 6
- conv_weight: float32 [3, 3, 1024], replicated, may hold values from -2 to 2
- conv_bias: float32 [1024], replicated, may hold values from -2.5 to 2.5
Outputs:
- block_out: bfloat16 [256, 256, 1024], P('ht', 'wt')
The draws below stay inside these ranges and needn't reach their ends.
Inputs may be any that keep to these rules, and one draw needn't show every extreme that they name: `keys_new`: key features. `keys_cache`: key features.
All inputs are finite; a program needn't handle non-finite values.
Results may differ from the reference program's by a relative error of at most 0.003.
Values may be sent and summed in bfloat16 or wider, within the bound.
A program may use at most 64 MiB of HBM per device.

```python
import jax
import jax.numpy as jnp
from jax import lax

HD = 128
WIN = 32
CACHED = 1
CHANNELS = 1024
FRAME_H = 256
FRAME_W = 256


def draw_queries(key, part):
    noise_key = jax.random.fold_in(key, 5)
    drawn = 2.5 * jnp.clip(jax.random.normal(noise_key, (FRAME_H, FRAME_W, CHANNELS), jnp.float32), -6.0, 6.0)
    return drawn.astype(jnp.bfloat16)


def draw_keys_new(key, part):
    noise_key = jax.random.fold_in(key, 6)
    drawn = jnp.clip(jax.random.normal(noise_key, (FRAME_H, FRAME_W, CHANNELS), jnp.float32), -6.0, 6.0)
    return drawn.astype(jnp.bfloat16)


def draw_keys_cache(key, part):
    noise_key = jax.random.fold_in(key, 7)
    drawn = jnp.clip(jax.random.normal(noise_key, (CACHED, FRAME_H, FRAME_W, CHANNELS), jnp.float32), -6.0, 6.0)
    return drawn.astype(jnp.bfloat16)


def levels(rng, shape, shards, least, high):
    gain = 1.0
    for dim, blocks in shards:
        steps = jax.random.uniform(jax.random.fold_in(jax.random.fold_in(rng, 6), dim), (blocks,), jnp.float32, least / len(shards), high / len(shards))
        gain = gain * jnp.repeat(jnp.exp(steps), shape[dim] // blocks).reshape((-1,) + (1,) * (len(shape) - 1 - dim))
    return gain


def centred(rng, shape, scale, reach, pieces=(), kind=jnp.bfloat16):
    entries = jax.random.normal(rng, shape, jnp.float32) * scale
    if len(pieces) > 0:
        entries = levels(rng, shape, pieces, -0.22, 0.18) * entries
    return jnp.clip(entries, min=-reach, max=reach).astype(kind)


def setup_inputs(seed: int = 0) -> dict:
    key_list = jax.random.split(jax.random.key(seed), 8)
    return {
        "queries": draw_queries(jax.random.fold_in(key_list[7], 71), 0),
        "keys_new": draw_keys_new(jax.random.fold_in(key_list[7], 71), 0),
        "values_new": centred(key_list[2], (FRAME_H, FRAME_W, CHANNELS), 1.0, 6.0, ((0, 16), (1, 32))),
        "keys_cache": draw_keys_cache(jax.random.fold_in(key_list[7], 71), 0),
        "values_cache": centred(key_list[4], (CACHED, FRAME_H, FRAME_W, CHANNELS), 1.0, 6.0, ((1, 16), (2, 32))),
        "conv_weight": centred(key_list[5], (3, 3, CHANNELS), 0.35, 2.0, (), jnp.float32),
        "conv_bias": centred(key_list[6], (CHANNELS,), 0.5, 2.5, (), jnp.float32),
    }


def window_allowed(row_start, col_start, frame_rows, frame_cols, tile_rows, tile_cols, half_win):
    ext_rows = jnp.arange(tile_rows + 2 * half_win, dtype=jnp.int32) - half_win
    ext_cols = jnp.arange(tile_cols + 2 * half_win, dtype=jnp.int32) - half_win
    query_rows = jnp.arange(tile_rows, dtype=jnp.int32)
    query_cols = jnp.arange(tile_cols, dtype=jnp.int32)
    row_delta = ext_rows[None, :] - query_rows[:, None]
    col_delta = ext_cols[None, :] - query_cols[:, None]
    global_rows = row_start + ext_rows
    global_cols = col_start + ext_cols
    row_valid = (row_delta >= -half_win) & (row_delta < half_win) & ((global_rows >= 0) & (global_rows < frame_rows))[None, :]
    col_valid = (col_delta >= -half_win) & (col_delta < half_win) & ((global_cols >= 0) & (global_cols < frame_cols))[None, :]
    allowed = row_valid[:, None, :, None] & col_valid[None, :, None, :]
    return allowed.reshape(tile_rows * tile_cols, (tile_rows + 2 * half_win) * (tile_cols + 2 * half_win))


def attend(query_rows, keys_flat, values_flat, allowed, heads, head_dim):
    score_scale = head_dim ** -0.5

    def one_head(head_index):
        lane_start = head_index * head_dim
        query_head = lax.dynamic_slice_in_dim(query_rows, lane_start, head_dim, 1).astype(jnp.float32)
        key_head = lax.dynamic_slice_in_dim(keys_flat, lane_start, head_dim, 1).astype(jnp.float32)
        value_head = lax.dynamic_slice_in_dim(values_flat, lane_start, head_dim, 1)
        scores = jnp.einsum("qd,kd->qk", query_head, key_head) * score_scale
        scores = jnp.where(allowed, scores, -1e30)
        row_top = jnp.max(scores, axis=1, keepdims=True)
        weights_f = jnp.exp(scores - row_top)
        denominator = jnp.sum(weights_f, axis=1, keepdims=True)
        numerator = jnp.dot(weights_f.astype(jnp.bfloat16), value_head, preferred_element_type=jnp.float32)
        return numerator / denominator

    outputs = lax.map(one_head, jnp.arange(heads, dtype=jnp.int32))
    return outputs.transpose(1, 0, 2).reshape(query_rows.shape[0], heads * head_dim)


def local_conv(padded, conv_weight, conv_bias, tile_rows, tile_cols):
    enhanced = jnp.zeros((tile_rows, tile_cols, padded.shape[2]), jnp.float32) + conv_bias
    for row_shift in range(3):
        for col_shift in range(3):
            enhanced = enhanced + padded[row_shift:row_shift + tile_rows, col_shift:col_shift + tile_cols].astype(jnp.float32) * conv_weight[row_shift, col_shift]
    return enhanced


def reference(queries, keys_new, values_new, keys_cache, values_cache, conv_weight, conv_bias):
    frame_rows, frame_cols, channels = queries.shape
    frames = keys_cache.shape[0] + 1
    half_win = WIN // 2
    stacked = jnp.concatenate([keys_cache, keys_new[None], values_cache, values_new[None]], axis=0)
    padded_all = jnp.pad(stacked, ((0, 0), (half_win, half_win), (half_win, half_win), (0, 0)))
    padded_values = jnp.pad(values_new, ((1, 1), (1, 1), (0, 0)))
    block_cols = frame_cols // WIN
    block_count = (frame_rows // WIN) * block_cols
    zero_index = jnp.int32(0)

    def one_block(block):
        row_start = ((block // block_cols) * WIN).astype(jnp.int32)
        col_start = ((block % block_cols) * WIN).astype(jnp.int32)
        query_block = lax.dynamic_slice(queries, (row_start, col_start, zero_index), (WIN, WIN, channels))
        region = lax.dynamic_slice(padded_all, (zero_index, row_start, col_start, zero_index), (2 * frames, 2 * WIN, 2 * WIN, channels))
        keys_flat = region[:frames].reshape(frames * 4 * WIN * WIN, channels)
        values_flat = region[frames:].reshape(frames * 4 * WIN * WIN, channels)
        allowed = jnp.tile(window_allowed(row_start, col_start, frame_rows, frame_cols, WIN, WIN, half_win), (1, frames))
        attended = attend(query_block.reshape(WIN * WIN, channels), keys_flat, values_flat, allowed, channels // HD, HD)
        beside_all = lax.dynamic_slice(padded_values, (row_start, col_start, zero_index), (WIN + 2, WIN + 2, channels))
        enhanced = local_conv(beside_all, conv_weight, conv_bias, WIN, WIN)
        return (attended.reshape(WIN, WIN, channels) + enhanced).astype(jnp.bfloat16)

    blocks = lax.map(one_block, jnp.arange(block_count, dtype=jnp.int32))
    blocks = blocks.reshape(frame_rows // WIN, block_cols, WIN, WIN, channels)
    return blocks.transpose(0, 2, 1, 3, 4).reshape(frame_rows, frame_cols, channels)
```

```python
import functools

import jax
import jax.numpy as jnp
from jax import lax
from jax.experimental import pallas as pl
from jax.experimental.pallas import tpu as pltpu
from jax.sharding import PartitionSpec as P

MESH = pl.DeviceIdType.MESH
HD = 128
WIN = 32
HALF = WIN // 2
ROWS = 16
COLS = 8
TILE = ROWS * COLS
HEADS = 8
GROUP = HEADS // 2
KEYS = 3 * TILE
EDGE = 2 * ROWS
LOG2E = 1.4426950408889634
MASKED = -1e30


def iota(shape, dim):
    return lax.broadcasted_iota(jnp.int32, shape, dim)


def row_bias(chip, chips, t):
    q_row = iota((TILE, KEYS), 0) // COLS
    k_row = iota((TILE, KEYS), 1) // COLS - ROWS
    frame_row = k_row + (2 * chip + t) * ROWS
    delta = k_row - q_row
    return (delta >= -HALF) & (delta < HALF) & (frame_row >= 0) & (frame_row < chips * 2 * ROWS)


def kernel(
    chips, strips, q_ref, kc_ref, kn_ref, vc_ref, vn_ref, cw_ref, cb_ref, out_ref,
    src, qsrc, kv, qb, own_bias, far_bias, own_o, own_s, far_send, far_recv, stat_send, stat_recv, stage,
    load_sem, qload_sem, local_sem, qlocal_sem,
    z_send, y_send, sib_send, relay_send, q_send, qsib_send, o_send, s_send, out_send, out_local,
    kv_recv, q_recv, o_recv, s_recv, out_recv,
):
    ht = lax.axis_index("ht")
    wt = lax.axis_index("wt")
    chip, core = ht // 2, ht % 2
    strip, half = wt // 2, wt % 2
    other = 1 - core
    far = wt + 1 - 2 * half
    has_up, has_down = chip > 0, chip < chips - 1
    has_left, has_right = strip > 0, strip < strips - 1

    def remote(source, target, send_sem, recv_sem, to_ht, to_wt):
        return pltpu.make_async_remote_copy(
            src_ref=source, dst_ref=target, send_sem=send_sem, recv_sem=recv_sem,
            device_id={"ht": to_ht, "wt": to_wt}, device_id_type=MESH,
        )

    inputs = (kc_ref, kn_ref, vc_ref, vn_ref)
    order = [g * GROUP + i for i in range(GROUP) for g in range(2)]

    def load(head, a):
        lanes = pl.ds(head * HD, HD)
        return pltpu.make_async_copy(inputs[a].at[:, lanes], src.at[head, a], load_sem.at[head, a])

    def qload(head):
        return pltpu.make_async_copy(q_ref.at[:, pl.ds(head * HD, HD)], qsrc.at[head], qload_sem.at[head])

    for head in order:
        for a in range(4):
            load(head, a).start()
        qload(head).start()

    barrier = pltpu.get_barrier_semaphore()

    def greet(to_ht, to_wt):
        pl.semaphore_signal(barrier, inc=1, device_id={"ht": to_ht, "wt": to_wt}, device_id_type=MESH)

    greet(2 * chip + other, wt)
    for c in range(2):
        greet(2 * chip + c, far)

        @pl.when(has_up)
        def _():
            greet(2 * (chip - 1) + c, wt)

        @pl.when(has_down)
        def _():
            greet(2 * (chip + 1) + c, wt)

        @pl.when(has_left)
        def _():
            greet(2 * chip + c, wt - 2)

        @pl.when(has_right)
        def _():
            greet(2 * chip + c, wt + 2)

    def clear(s, r):
        @pl.loop(0, GROUP)
        def _(i):
            kv[i, s, r] = jnp.zeros((4, TILE, HD), jnp.bfloat16)

    @pl.when(jnp.logical_not(has_left))
    def _():
        for r in range(4):
            clear(0, r)

    @pl.when(jnp.logical_not(has_right))
    def _():
        for r in range(4):
            clear(2, r)

    @pl.when(jnp.logical_not(has_up))
    def _():
        for s in range(3):
            clear(s, 0)

    @pl.when(jnp.logical_not(has_down))
    def _():
        for s in range(3):
            clear(s, 3)

    for head in order:
        for a in range(4):
            load(head, a).wait()
        qload(head).wait()

    greeted = 3 + 2 * (
        has_up.astype(jnp.int32) + has_down.astype(jnp.int32) + has_left.astype(jnp.int32) + has_right.astype(jnp.int32)
    )
    pl.semaphore_wait(barrier, greeted)

    sends_z = jnp.where(core == 1, chip < chips - 1, chip > 0)
    z_chip = jnp.where(core == 1, jnp.minimum(chip + 1, chips - 1), jnp.maximum(chip - 1, 0))
    z_slot = 3 * other

    def z_copy(i, c):
        return remote(
            src.at[c * GROUP + i], kv.at[i, 1, z_slot], z_send.at[i, c], kv_recv.at[i, 1, z_slot], 2 * z_chip + c, wt
        )

    def sib_copy(i):
        return remote(
            src.at[other * GROUP + i], kv.at[i, 1, 1 + core], sib_send.at[i], kv_recv.at[i, 1, 1 + core],
            2 * chip + other, wt,
        )

    def own_copy(i):
        return pltpu.make_async_copy(src.at[core * GROUP + i], kv.at[i, 1, 1 + core], local_sem.at[i])

    sides = ((has_left, -2, 2), (has_right, 2, 0))

    def y_copy(i, d, c):
        _, step, s = sides[d]
        return remote(
            src.at[c * GROUP + i], kv.at[i, s, 1 + core], y_send.at[i, d, c], kv_recv.at[i, s, 1 + core],
            2 * chip + c, wt + step,
        )

    def relay_copy(i, d, n):
        _, step, s = sides[d]
        return remote(
            kv.at[i, 1, 3 * n], kv.at[i, s, 3 * n], relay_send.at[i, d, n], kv_recv.at[i, s, 3 * n], ht, wt + step
        )

    def q_copy(i, c):
        return remote(
            qsrc.at[c * GROUP + i], qb.at[i, 1, core], q_send.at[i, c], q_recv.at[i, 1, core], 2 * chip + c, far
        )

    def qsib_copy(i):
        return remote(
            qsrc.at[other * GROUP + i], qb.at[i, 0, core], qsib_send.at[i], q_recv.at[i, 0, core],
            2 * chip + other, wt,
        )

    def qown_copy(i):
        return pltpu.make_async_copy(qsrc.at[core * GROUP + i], qb.at[i, 0, core], qlocal_sem.at[i])

    def kv_arrived(i, s, r):
        pltpu.make_async_copy(src.at[0], kv.at[i, s, r], kv_recv.at[i, s, r]).wait()

    for i in range(GROUP):
        @pl.when(sends_z)
        def _():
            for c in range(2):
                z_copy(i, c).start()

    for i in range(GROUP):
        sib_copy(i).start()
        own_copy(i).start()
        qsib_copy(i).start()
        qown_copy(i).start()
        for c in range(2):
            q_copy(i, c).start()

    ends = (has_up, has_down)
    for i in range(GROUP):
        for d in range(2):
            @pl.when(sides[d][0])
            def _():
                for c in range(2):
                    y_copy(i, d, c).start()

        if i == 0:
            for t in range(2):
                rows = row_bias(chip, chips, t)
                q_col = iota((TILE, KEYS), 0) % COLS
                k_col = iota((TILE, KEYS), 1) % COLS
                for s in range(3):
                    delta = k_col - q_col + (s - 1) * 2 * COLS
                    inside = (strip + s - 1 >= 0) & (strip + s - 1 < strips)
                    ok = rows & (delta >= -HALF) & (delta < HALF)
                    own_bias[t, s] = jnp.where(ok & inside, 0.0, MASKED)
                for n in range(2):
                    at = strip + n - half
                    far_bias[t, n] = jnp.where(rows & (at >= 0) & (at < strips), 0.0, MASKED)

        for n in range(2):
            @pl.when(ends[n])
            def _():
                kv_arrived(i, 1, 3 * n)
                for d in range(2):
                    @pl.when(sides[d][0])
                    def _():
                        relay_copy(i, d, n).start()

    eye = iota((TILE, TILE), 0) == iota((TILE, TILE), 1)

    def attend(q, i, t, blocks):
        scores = []
        for s, bias in blocks:
            for f in range(2):
                k = kv[i, s, pl.ds(t, 3), f].reshape(KEYS, HD)
                dots = lax.dot_general(q, k, (((1,), (1,)), ((), ())), preferred_element_type=jnp.float32)
                scores.append(dots * (HD**-0.5 * LOG2E) + bias[...])
        top = functools.reduce(jnp.maximum, scores)
        top = jnp.max(top, axis=1, keepdims=True)
        total = jnp.zeros((TILE, KEYS), jnp.float32)
        acc = jnp.zeros((TILE, HD), jnp.float32)
        n = 0
        for s, _ in blocks:
            for f in range(2):
                weights = jnp.exp2(scores[n] - top)
                total = total + weights
                v = kv[i, s, pl.ds(t, 3), 2 + f].reshape(KEYS, HD)
                acc = acc + jnp.dot(weights.astype(jnp.bfloat16), v, preferred_element_type=jnp.float32)
                n += 1
        total = jnp.sum(total, axis=1, keepdims=True)
        return acc * (1.0 / total), top + jnp.log2(total)

    def taps(i):
        lanes = pl.ds(pl.multiple_of((core * GROUP + i) * HD, HD), HD)
        return [[cw_ref[pl.ds(3 * a + b, 1), lanes] for b in range(3)] for a in range(3)], cb_ref[:, lanes]

    def edges(i, t):
        weight, _ = taps(i)
        pick = iota((3 * ROWS, KEYS), 0)
        key = iota((3 * ROWS, KEYS), 1)
        wanted = (ROWS - 1 + pick % ROWS + pick // ROWS) * COLS
        parts = []
        for n, col, b in ((0, COLS - 1, 0), (1, 0, 2)):
            v = kv[i, 1 - half + n, pl.ds(t, 3), 3].reshape(KEYS, HD)
            chosen = jnp.where(key == wanted + col, 1.0, 0.0).astype(jnp.bfloat16)
            picked = jnp.dot(chosen, v, preferred_element_type=jnp.float32)
            parts.append(sum(picked[a * ROWS : (a + 1) * ROWS] * weight[a][b] for a in range(3)))
        return jnp.concatenate(parts, axis=0).astype(jnp.bfloat16)

    def conv(i, t):
        weight, bias = taps(i)
        v = kv[i, 1, pl.ds(t, 3), 3].reshape(KEYS, HD).astype(jnp.float32)
        rows = [v[TILE + (a - 1) * COLS : 2 * TILE + (a - 1) * COLS] for a in range(3)]
        left, here, right = (sum(rows[a] * weight[a][b] for a in range(3)) for b in range(3))
        col = iota((TILE, HD), 0) % COLS
        left = jnp.where(col == 0, 0.0, pltpu.roll(left, 1, 0))
        right = jnp.where(col == COLS - 1, 0.0, pltpu.roll(right, TILE - 1, 0))
        return here + left + right + bias

    def o_copy(i):
        return remote(far_send.at[i], far_recv.at[i], o_send.at[i], o_recv.at[i], ht, far)

    def s_copy(i):
        return remote(stat_send.at[i], stat_recv.at[i], s_send.at[i], s_recv.at[i], ht, far)

    def wait_inputs(i):
        own_copy(i).wait()
        qown_copy(i).wait()
        kv_arrived(i, 1, 1 + other)
        pltpu.make_async_copy(qsrc.at[0], qb.at[i, 0, other], q_recv.at[i, 0, other]).wait()
        for t in range(2):
            pltpu.make_async_copy(qsrc.at[0], qb.at[i, 1, t], q_recv.at[i, 1, t]).wait()
        for valid, s in ((has_left, 0), (has_right, 2)):
            @pl.when(valid)
            def _():
                kv_arrived(i, s, 1)
                kv_arrived(i, s, 2)

                @pl.when(has_up)
                def _():
                    kv_arrived(i, s, 0)

                @pl.when(has_down)
                def _():
                    kv_arrived(i, s, 3)

    @pl.loop(0, GROUP)
    def _(i):
        wait_inputs(i)

        @pl.loop(0, 2)
        def _(t):
            o, s = attend(qb[i, 1, t], i, t, [(1 - half + n, far_bias.at[t, n]) for n in range(2)])
            far_send[i, t, :TILE] = o.astype(jnp.bfloat16)
            far_send[i, t, TILE:] = edges(i, t)
            stat_send[i, pl.ds(t, 1)] = jnp.sum(jnp.where(eye, s, 0.0), axis=0, keepdims=True)

        o_copy(i).start()
        s_copy(i).start()

        @pl.loop(0, 2)
        def _(t):
            o, s = attend(qb[i, 0, t], i, t, [(n, own_bias.at[t, n]) for n in range(3)])
            own_o[i, t] = o
            own_s[i, t] = jnp.broadcast_to(s, (TILE, HD))

    def out_lanes(i):
        return out_ref.at[:, pl.ds(pl.multiple_of((core * GROUP + i) * HD, HD), HD)]

    def out_own(i):
        return pltpu.make_async_copy(stage.at[i, core], out_lanes(i), out_local.at[i])

    def out_sib(i):
        return remote(stage.at[i, other], out_lanes(i), out_send.at[i], out_recv.at[i], 2 * chip + other, wt)

    @pl.loop(0, GROUP)
    def _(i):
        o_copy(i).wait_recv()
        s_copy(i).wait_recv()

        @pl.loop(0, 2)
        def _(t):
            far_s = jnp.sum(jnp.where(eye, stat_recv[i, pl.ds(t, 1)], 0.0), axis=1, keepdims=True)
            shift = far_s - own_s[i, t]
            own_w = 1.0 / (1.0 + jnp.exp2(shift))
            far_w = 1.0 / (1.0 + jnp.exp2(-shift))
            place = iota((TILE, EDGE), 0)
            edge = iota((TILE, EDGE), 1)
            spot = (edge % ROWS) * COLS + (edge // ROWS) * (COLS - 1)
            spread = jnp.where(place == spot, 1.0, 0.0).astype(jnp.bfloat16)
            edge_part = jnp.dot(spread, far_recv[i, t, TILE:], preferred_element_type=jnp.float32)
            mixed = own_o[i, t] * own_w + far_recv[i, t, :TILE].astype(jnp.float32) * far_w
            stage[i, t] = (mixed + (conv(i, t) + edge_part)).astype(jnp.bfloat16)

        out_sib(i).start()
        out_own(i).start()

    for i in range(GROUP):
        @pl.when(sends_z)
        def _():
            for c in range(2):
                z_copy(i, c).wait_send()

        sib_copy(i).wait_send()
        qsib_copy(i).wait_send()
        for c in range(2):
            q_copy(i, c).wait_send()
        for d in range(2):
            @pl.when(sides[d][0])
            def _():
                for c in range(2):
                    y_copy(i, d, c).wait_send()
                for n in range(2):
                    @pl.when(ends[n])
                    def _():
                        relay_copy(i, d, n).wait_send()

        o_copy(i).wait_send()
        s_copy(i).wait_send()
        out_sib(i).wait_send()
        out_own(i).wait()
        pltpu.make_async_copy(
            stage.at[i, 0],
            out_ref.at[:, pl.ds(pl.multiple_of((other * GROUP + i) * HD, HD), HD)],
            out_recv.at[i],
        ).wait()


def shards(chips, strips, queries, keys_new, values_new, keys_cache, values_cache, conv_weight, conv_bias):
    rows, cols, channels = queries.shape
    flat = [x.reshape(TILE, channels) for x in (queries, keys_cache, keys_new, values_cache, values_new)]
    any_spec = pl.BlockSpec(memory_space=pl.ANY)
    vmem_spec = pl.BlockSpec(memory_space=pltpu.VMEM)
    bf16, f32 = jnp.bfloat16, jnp.float32
    dma = pltpu.SemaphoreType.DMA
    out = pl.pallas_call(
        functools.partial(kernel, chips, strips),
        out_shape=jax.ShapeDtypeStruct((TILE, channels), bf16),
        in_specs=[any_spec] * 5 + [vmem_spec] * 2,
        out_specs=any_spec,
        scratch_shapes=[
            pltpu.VMEM((HEADS, 4, TILE, HD), bf16),
            pltpu.VMEM((HEADS, TILE, HD), bf16),
            pltpu.VMEM((GROUP, 3, 4, 4, TILE, HD), bf16),
            pltpu.VMEM((GROUP, 2, 2, TILE, HD), bf16),
            pltpu.VMEM((2, 3, TILE, KEYS), f32),
            pltpu.VMEM((2, 2, TILE, KEYS), f32),
            pltpu.VMEM((GROUP, 2, TILE, HD), f32),
            pltpu.VMEM((GROUP, 2, TILE, HD), f32),
            pltpu.VMEM((GROUP, 2, TILE + EDGE, HD), bf16),
            pltpu.VMEM((GROUP, 2, TILE + EDGE, HD), bf16),
            pltpu.VMEM((GROUP, 2, HD), f32),
            pltpu.VMEM((GROUP, 2, HD), f32),
            pltpu.VMEM((GROUP, 2, TILE, HD), bf16),
            dma((HEADS, 4)), dma((HEADS,)), dma((GROUP,)), dma((GROUP,)),
            dma((GROUP, 2)), dma((GROUP, 2, 2)), dma((GROUP,)), dma((GROUP, 2, 2)), dma((GROUP, 2)), dma((GROUP,)),
            dma((GROUP,)), dma((GROUP,)), dma((GROUP,)), dma((GROUP,)),
            dma((GROUP, 3, 4)), dma((GROUP, 2, 2)), dma((GROUP,)), dma((GROUP,)), dma((GROUP,)),
        ],
        compiler_params=pltpu.CompilerParams(
            collective_id=0, has_side_effects=True, vmem_limit_bytes=56 << 20
        ),
    )(*flat, conv_weight.reshape(9, channels), conv_bias.reshape(1, channels))
    return out.reshape(rows, cols, channels)


def solution(mesh):
    placed = (
        P("ht", "wt", None),
        P("ht", "wt", None),
        P("ht", "wt", None),
        P(None, "ht", "wt", None),
        P(None, "ht", "wt", None),
        P(),
        P(),
    )
    body = functools.partial(shards, mesh.shape["ht"] // 2, mesh.shape["wt"] // 2)
    return jax.shard_map(body, mesh=mesh, in_specs=placed, out_specs=P("ht", "wt", None), check_vma=False)
```

```python
import functools

import jax
import jax.numpy as jnp
from jax import lax
from jax.experimental import pallas as pl
from jax.experimental.pallas import tpu as pltpu
from jax.sharding import PartitionSpec as P

MESH = pl.DeviceIdType.MESH
HD = 128
WIN = 32
HALF = WIN // 2
ROWS = 16
COLS = 8
TILE = ROWS * COLS
HEADS = 8
GROUP = HEADS // 2
KEYS = 3 * TILE
EDGE = 2 * ROWS
LOG2E = 1.4426950408889634
MASKED = -1e30


def iota(shape, dim):
    return lax.broadcasted_iota(jnp.int32, shape, dim)


def row_bias(chip, chips, t):
    q_row = iota((TILE, KEYS), 0) // COLS
    k_row = iota((TILE, KEYS), 1) // COLS - ROWS
    frame_row = k_row + (2 * chip + t) * ROWS
    delta = k_row - q_row
    return (delta >= -HALF) & (delta < HALF) & (frame_row >= 0) & (frame_row < chips * 2 * ROWS)


def kernel(
    chips, strips, q_ref, kc_ref, kn_ref, vc_ref, vn_ref, cw_ref, cb_ref, out_ref,
    src, qsrc, kv, qb, own_bias, far_bias, own, sib_in, far_send, far_recv, stat_send, stat_recv,
    load_sem, qload_sem, local_sem, qlocal_sem,
    z_send, y_send, sib_send, relay_send, q_send, qsib_send, o_send, s_send, own_send,
    kv_recv, q_recv, o_recv, s_recv, own_recv,
):
    ht = lax.axis_index("ht")
    wt = lax.axis_index("wt")
    chip, core = ht // 2, ht % 2
    strip, half = wt // 2, wt % 2
    other = 1 - core
    far = wt + 1 - 2 * half
    has_up, has_down = chip > 0, chip < chips - 1
    has_left, has_right = strip > 0, strip < strips - 1

    def remote(source, target, send_sem, recv_sem, to_ht, to_wt):
        return pltpu.make_async_remote_copy(
            src_ref=source, dst_ref=target, send_sem=send_sem, recv_sem=recv_sem,
            device_id={"ht": to_ht, "wt": to_wt}, device_id_type=MESH,
        )

    inputs = (kc_ref, kn_ref, vc_ref, vn_ref)
    order = [g * GROUP + i for i in range(GROUP) for g in range(2)]

    def load(head, a):
        lanes = pl.ds(head * HD, HD)
        return pltpu.make_async_copy(inputs[a].at[:, lanes], src.at[head, a], load_sem.at[head, a])

    def qload(head):
        return pltpu.make_async_copy(q_ref.at[:, pl.ds(head * HD, HD)], qsrc.at[head], qload_sem.at[head])

    barrier = pltpu.get_barrier_semaphore()

    def greet(to_ht, to_wt):
        pl.semaphore_signal(barrier, inc=1, device_id={"ht": to_ht, "wt": to_wt}, device_id_type=MESH)

    greet(2 * chip + other, wt)
    for c in range(2):
        greet(2 * chip + c, far)

        @pl.when(has_up)
        def _():
            greet(2 * (chip - 1) + c, wt)

        @pl.when(has_down)
        def _():
            greet(2 * (chip + 1) + c, wt)

        @pl.when(has_left)
        def _():
            greet(2 * chip + c, wt - 2)

        @pl.when(has_right)
        def _():
            greet(2 * chip + c, wt + 2)

    for head in order:
        for a in range(4):
            load(head, a).start()
        qload(head).start()

    def clear(s, r):
        @pl.loop(0, GROUP)
        def _(i):
            kv[i, s, r] = jnp.zeros((4, TILE, HD), jnp.bfloat16)

    @pl.when(jnp.logical_not(has_left))
    def _():
        for r in range(4):
            clear(0, r)

    @pl.when(jnp.logical_not(has_right))
    def _():
        for r in range(4):
            clear(2, r)

    @pl.when(jnp.logical_not(has_up))
    def _():
        for s in range(3):
            clear(s, 0)

    @pl.when(jnp.logical_not(has_down))
    def _():
        for s in range(3):
            clear(s, 3)

    for head in order:
        for a in range(4):
            load(head, a).wait()
        qload(head).wait()

    greeted = 3 + 2 * (
        has_up.astype(jnp.int32) + has_down.astype(jnp.int32) + has_left.astype(jnp.int32) + has_right.astype(jnp.int32)
    )
    pl.semaphore_wait(barrier, greeted)

    sends_z = jnp.where(core == 1, chip < chips - 1, chip > 0)
    z_chip = jnp.where(core == 1, jnp.minimum(chip + 1, chips - 1), jnp.maximum(chip - 1, 0))
    z_slot = 3 * other

    def z_copy(i, c):
        return remote(
            src.at[c * GROUP + i], kv.at[i, 1, z_slot], z_send.at[i, c], kv_recv.at[i, 1, z_slot], 2 * z_chip + c, wt
        )

    def sib_copy(i):
        return remote(
            src.at[other * GROUP + i], kv.at[i, 1, 1 + core], sib_send.at[i], kv_recv.at[i, 1, 1 + core],
            2 * chip + other, wt,
        )

    def own_copy(i):
        return pltpu.make_async_copy(src.at[core * GROUP + i], kv.at[i, 1, 1 + core], local_sem.at[i])

    sides = ((has_left, -2, 2), (has_right, 2, 0))

    def y_copy(i, d, c):
        _, step, s = sides[d]
        return remote(
            src.at[c * GROUP + i], kv.at[i, s, 1 + core], y_send.at[i, d, c], kv_recv.at[i, s, 1 + core],
            2 * chip + c, wt + step,
        )

    def relay_copy(i, d, n):
        _, step, s = sides[d]
        return remote(
            kv.at[i, 1, 3 * n], kv.at[i, s, 3 * n], relay_send.at[i, d, n], kv_recv.at[i, s, 3 * n], ht, wt + step
        )

    def q_copy(i, c):
        return remote(
            qsrc.at[c * GROUP + i], qb.at[i, 1, core], q_send.at[i, c], q_recv.at[i, 1, core], 2 * chip + c, far
        )

    def qsib_copy(i):
        return remote(
            qsrc.at[other * GROUP + i], qb.at[i, 0, core], qsib_send.at[i], q_recv.at[i, 0, core],
            2 * chip + other, wt,
        )

    def qown_copy(i):
        return pltpu.make_async_copy(qsrc.at[core * GROUP + i], qb.at[i, 0, core], qlocal_sem.at[i])

    def kv_arrived(i, s, r):
        pltpu.make_async_copy(src.at[0], kv.at[i, s, r], kv_recv.at[i, s, r]).wait()

    for i in range(GROUP):
        @pl.when(sends_z)
        def _():
            for c in range(2):
                z_copy(i, c).start()

        if i > 0:
            for c in range(2):
                q_copy(i - 1, c).start()

    for c in range(2):
        q_copy(GROUP - 1, c).start()

    for i in range(GROUP):
        sib_copy(i).start()
        own_copy(i).start()
        qsib_copy(i).start()
        qown_copy(i).start()

    ends = (has_up, has_down)
    for i in range(GROUP):
        for d in range(2):
            @pl.when(sides[d][0])
            def _():
                for c in range(2):
                    y_copy(i, d, c).start()

        if i == 0:
            for t in range(2):
                rows = row_bias(chip, chips, t)
                q_col = iota((TILE, KEYS), 0) % COLS
                k_col = iota((TILE, KEYS), 1) % COLS
                for s in range(3):
                    delta = k_col - q_col + (s - 1) * 2 * COLS
                    inside = (strip + s - 1 >= 0) & (strip + s - 1 < strips)
                    ok = rows & (delta >= -HALF) & (delta < HALF)
                    own_bias[t, s] = jnp.where(ok & inside, 0.0, MASKED)
                for n in range(2):
                    at = strip + n - half
                    far_bias[t, n] = jnp.where(rows & (at >= 0) & (at < strips), 0.0, MASKED)

        for n in range(2):
            @pl.when(ends[n])
            def _():
                kv_arrived(i, 1, 3 * n)
                for d in range(2):
                    @pl.when(sides[d][0])
                    def _():
                        relay_copy(i, d, n).start()

    eye = iota((TILE, TILE), 0) == iota((TILE, TILE), 1)

    def attend(q, i, t, blocks):
        scores = []
        for s, bias in blocks:
            for f in range(2):
                k = kv[i, s, pl.ds(t, 3), f].reshape(KEYS, HD)
                dots = lax.dot_general(q, k, (((1,), (1,)), ((), ())), preferred_element_type=jnp.float32)
                scores.append(dots * (HD**-0.5 * LOG2E) + bias[...])
        top = functools.reduce(jnp.maximum, scores)
        top = jnp.max(top, axis=1, keepdims=True)
        total = jnp.zeros((TILE, KEYS), jnp.float32)
        acc = jnp.zeros((TILE, HD), jnp.float32)
        n = 0
        for s, _ in blocks:
            for f in range(2):
                weights = jnp.exp2(scores[n] - top)
                total = total + weights
                v = kv[i, s, pl.ds(t, 3), 2 + f].reshape(KEYS, HD)
                acc = acc + jnp.dot(weights.astype(jnp.bfloat16), v, preferred_element_type=jnp.float32)
                n += 1
        total = jnp.sum(total, axis=1, keepdims=True)
        return acc * (1.0 / total), top + jnp.log2(total)

    def taps(i):
        lanes = pl.ds(pl.multiple_of((core * GROUP + i) * HD, HD), HD)
        return [[cw_ref[a, pl.ds(b, 1), lanes] for b in range(3)] for a in range(3)], cb_ref[:, lanes]

    def edges(i, t):
        weight, _ = taps(i)
        pick = iota((3 * ROWS, KEYS), 0)
        key = iota((3 * ROWS, KEYS), 1)
        wanted = (ROWS - 1 + pick % ROWS + pick // ROWS) * COLS
        parts = []
        for n, col, b in ((0, COLS - 1, 0), (1, 0, 2)):
            v = kv[i, 1 - half + n, pl.ds(t, 3), 3].reshape(KEYS, HD)
            chosen = jnp.where(key == wanted + col, 1.0, 0.0).astype(jnp.bfloat16)
            picked = jnp.dot(chosen, v, preferred_element_type=jnp.float32)
            parts.append(sum(picked[a * ROWS : (a + 1) * ROWS] * weight[a][b] for a in range(3)))
        return jnp.concatenate(parts, axis=0).astype(jnp.bfloat16)

    def conv(i, t):
        weight, bias = taps(i)
        v = kv[i, 1, pl.ds(t, 3), 3].reshape(KEYS, HD).astype(jnp.float32)
        rows = [v[TILE + (a - 1) * COLS : 2 * TILE + (a - 1) * COLS] for a in range(3)]
        left, here, right = (sum(rows[a] * weight[a][b] for a in range(3)) for b in range(3))
        col = iota((TILE, HD), 0) % COLS
        left = jnp.where(col == 0, 0.0, pltpu.roll(left, 1, 0))
        right = jnp.where(col == COLS - 1, 0.0, pltpu.roll(right, TILE - 1, 0))
        return here + left + right + bias

    def o_copy(i, t):
        return remote(
            far_send.at[i, t], far_recv.at[core, i], o_send.at[i, t], o_recv.at[core, i], 2 * chip + t, far
        )

    def s_copy(i, t):
        return remote(
            stat_send.at[i, t], stat_recv.at[core, i], s_send.at[i, t], s_recv.at[core, i], 2 * chip + t, far
        )

    def own_part_copy(i):
        return remote(own.at[i, other], sib_in.at[i], own_send.at[i], own_recv.at[i], 2 * chip + other, wt)

    def wait_inputs(i):
        own_copy(i).wait()
        qown_copy(i).wait()
        kv_arrived(i, 1, 1 + other)
        pltpu.make_async_copy(qsrc.at[0], qb.at[i, 0, other], q_recv.at[i, 0, other]).wait()
        for t in range(2):
            pltpu.make_async_copy(qsrc.at[0], qb.at[i, 1, t], q_recv.at[i, 1, t]).wait()
        for valid, s in ((has_left, 0), (has_right, 2)):
            @pl.when(valid)
            def _():
                kv_arrived(i, s, 1)
                kv_arrived(i, s, 2)

                @pl.when(has_up)
                def _():
                    kv_arrived(i, s, 0)

                @pl.when(has_down)
                def _():
                    kv_arrived(i, s, 3)

    @pl.loop(0, GROUP)
    def _(i):
        wait_inputs(i)

        @pl.loop(0, 2)
        def _(t):
            o, s = attend(qb[i, 1, t], i, t, [(1 - half + n, far_bias.at[t, n]) for n in range(2)])
            far_send[i, t, :TILE] = o.astype(jnp.bfloat16)
            far_send[i, t, TILE:] = edges(i, t)
            stat_send[i, t] = jnp.sum(jnp.where(eye, s, 0.0), axis=0, keepdims=True)
            s_copy(i, t).start()
            o_copy(i, t).start()

        @pl.loop(0, 2)
        def _(t):
            o, s = attend(qb[i, 0, t], i, t, [(n, own_bias.at[t, n]) for n in range(3)])
            own[i, t, 0] = o
            own[i, t, 1] = conv(i, t)
            own[i, t, 2] = jnp.broadcast_to(s, (TILE, HD))

        own_part_copy(i).start()

    def complete(i, g, mine):
        pltpu.make_async_copy(stat_send.at[i, 0], stat_recv.at[g, i], s_recv.at[g, i]).wait()
        far_s = jnp.sum(jnp.where(eye, stat_recv[g, i], 0.0), axis=1, keepdims=True)
        shift = far_s - mine[2]
        own_w = 1.0 / (1.0 + jnp.exp2(shift))
        far_w = 1.0 / (1.0 + jnp.exp2(-shift))
        here = mine[0] * own_w + mine[1]
        place = iota((TILE, EDGE), 0)
        edge = iota((TILE, EDGE), 1)
        spot = (edge % ROWS) * COLS + (edge // ROWS) * (COLS - 1)
        spread = jnp.where(place == spot, 1.0, 0.0).astype(jnp.bfloat16)
        pltpu.make_async_copy(far_send.at[i, 0], far_recv.at[g, i], o_recv.at[g, i]).wait()
        edge_part = jnp.dot(spread, far_recv[g, i, TILE:], preferred_element_type=jnp.float32)
        there = far_recv[g, i, :TILE].astype(jnp.float32) * far_w
        lanes = pl.ds(pl.multiple_of((g * GROUP + i) * HD, HD), HD)
        out_ref[:, lanes] = (here + there + edge_part).astype(jnp.bfloat16)

    @pl.loop(0, GROUP)
    def _(i):
        pltpu.make_async_copy(own.at[i, 0], sib_in.at[i], own_recv.at[i]).wait()
        complete(i, core, own.at[i, core])
        complete(i, other, sib_in.at[i])

    for i in range(GROUP):
        @pl.when(sends_z)
        def _():
            for c in range(2):
                z_copy(i, c).wait_send()

        sib_copy(i).wait_send()
        qsib_copy(i).wait_send()
        for c in range(2):
            q_copy(i, c).wait_send()
        for d in range(2):
            @pl.when(sides[d][0])
            def _():
                for c in range(2):
                    y_copy(i, d, c).wait_send()
                for n in range(2):
                    @pl.when(ends[n])
                    def _():
                        relay_copy(i, d, n).wait_send()

        for t in range(2):
            o_copy(i, t).wait_send()
            s_copy(i, t).wait_send()
        own_part_copy(i).wait_send()


def shards(chips, strips, queries, keys_new, values_new, keys_cache, values_cache, conv_weight, conv_bias):
    rows, cols, channels = queries.shape
    flat = [x.reshape(TILE, channels) for x in (queries, keys_cache, keys_new, values_cache, values_new)]
    any_spec = pl.BlockSpec(memory_space=pl.ANY)
    vmem_spec = pl.BlockSpec(memory_space=pltpu.VMEM)
    bf16, f32 = jnp.bfloat16, jnp.float32
    dma = pltpu.SemaphoreType.DMA
    out = pl.pallas_call(
        functools.partial(kernel, chips, strips),
        out_shape=pltpu.VMEM((TILE, channels), bf16),
        in_specs=[any_spec] * 5 + [vmem_spec] * 2,
        out_specs=vmem_spec,
        scratch_shapes=[
            pltpu.VMEM((HEADS, 4, TILE, HD), bf16),
            pltpu.VMEM((HEADS, TILE, HD), bf16),
            pltpu.VMEM((GROUP, 3, 4, 4, TILE, HD), bf16),
            pltpu.VMEM((GROUP, 2, 2, TILE, HD), bf16),
            pltpu.VMEM((2, 3, TILE, KEYS), f32),
            pltpu.VMEM((2, 2, TILE, KEYS), f32),
            pltpu.VMEM((GROUP, 2, 3, TILE, HD), f32),
            pltpu.VMEM((GROUP, 3, TILE, HD), f32),
            pltpu.VMEM((GROUP, 2, TILE + EDGE, HD), bf16),
            pltpu.VMEM((2, GROUP, TILE + EDGE, HD), bf16),
            pltpu.VMEM((GROUP, 2, 1, HD), f32),
            pltpu.VMEM((2, GROUP, 1, HD), f32),
            dma((HEADS, 4)), dma((HEADS,)), dma((GROUP,)), dma((GROUP,)),
            dma((GROUP, 2)), dma((GROUP, 2, 2)), dma((GROUP,)), dma((GROUP, 2, 2)), dma((GROUP, 2)), dma((GROUP,)),
            dma((GROUP, 2)), dma((GROUP, 2)), dma((GROUP,)),
            dma((GROUP, 3, 4)), dma((GROUP, 2, 2)), dma((2, GROUP)), dma((2, GROUP)), dma((GROUP,)),
        ],
        compiler_params=pltpu.CompilerParams(
            collective_id=0, has_side_effects=True, vmem_limit_bytes=56 << 20
        ),
    )(*flat, conv_weight, conv_bias.reshape(1, channels))
    return out.reshape(rows, cols, channels)


def solution(mesh):
    placed = (
        P("ht", "wt", None),
        P("ht", "wt", None),
        P("ht", "wt", None),
        P(None, "ht", "wt", None),
        P(None, "ht", "wt", None),
        P(),
        P(),
    )
    body = functools.partial(shards, mesh.shape["ht"] // 2, mesh.shape["wt"] // 2)
    return jax.shard_map(body, mesh=mesh, in_specs=placed, out_specs=P("ht", "wt", None), check_vma=False)
```

```python
import functools

import jax
import jax.numpy as jnp
from jax import lax
from jax.experimental import pallas as pl
from jax.experimental.pallas import tpu as pltpu
from jax.sharding import PartitionSpec as P

MESH = pl.DeviceIdType.MESH
HD = 128
WIN = 32
HALF = WIN // 2
ROWS = 16
COLS = 8
TILE = ROWS * COLS
HEADS = 8
GROUP = HEADS // 2
KEYS = 3 * TILE
EDGE = 2 * ROWS
LOG2E = 1.4426950408889634
MASKED = -1e30


def iota(shape, dim):
    return lax.broadcasted_iota(jnp.int32, shape, dim)


def row_bias(chip, chips, t):
    q_row = iota((TILE, KEYS), 0) // COLS
    k_row = iota((TILE, KEYS), 1) // COLS - ROWS
    frame_row = k_row + (2 * chip + t) * ROWS
    delta = k_row - q_row
    return (delta >= -HALF) & (delta < HALF) & (frame_row >= 0) & (frame_row < chips * 2 * ROWS)


def kernel(
    chips, strips, q_ref, kc_ref, kn_ref, vc_ref, vn_ref, cw_ref, cb_ref, out_ref,
    src, qsrc, kv, qb, own_bias, far_bias, own, sib_in, far_send, far_recv, stat_send, stat_recv,
    load_sem, qload_sem, local_sem, qlocal_sem,
    z_send, y_send, sib_send, relay_send, q_send, qsib_send, o_send, s_send, own_send,
    kv_recv, q_recv, o_recv, s_recv, own_recv,
):
    ht = lax.axis_index("ht")
    wt = lax.axis_index("wt")
    chip, core = ht // 2, ht % 2
    strip, half = wt // 2, wt % 2
    other = 1 - core
    far = wt + 1 - 2 * half
    has_up, has_down = chip > 0, chip < chips - 1
    has_left, has_right = strip > 0, strip < strips - 1

    def remote(source, target, send_sem, recv_sem, to_ht, to_wt):
        return pltpu.make_async_remote_copy(
            src_ref=source, dst_ref=target, send_sem=send_sem, recv_sem=recv_sem,
            device_id={"ht": to_ht, "wt": to_wt}, device_id_type=MESH,
        )

    inputs = (kc_ref, kn_ref, vc_ref, vn_ref)
    order = [g * GROUP + i for i in range(GROUP) for g in range(2)]

    def load(head, a):
        lanes = pl.ds(head * HD, HD)
        return pltpu.make_async_copy(inputs[a].at[:, lanes], src.at[head, a], load_sem.at[head, a])

    def qload(head):
        return pltpu.make_async_copy(q_ref.at[:, pl.ds(head * HD, HD)], qsrc.at[head], qload_sem.at[head])

    barrier = pltpu.get_barrier_semaphore()

    def greet(to_ht, to_wt):
        pl.semaphore_signal(barrier, inc=1, device_id={"ht": to_ht, "wt": to_wt}, device_id_type=MESH)

    greet(2 * chip + other, wt)
    for c in range(2):
        greet(2 * chip + c, far)

        @pl.when(has_up)
        def _():
            greet(2 * (chip - 1) + c, wt)

        @pl.when(has_down)
        def _():
            greet(2 * (chip + 1) + c, wt)

        @pl.when(has_left)
        def _():
            greet(2 * chip + c, wt - 2)

        @pl.when(has_right)
        def _():
            greet(2 * chip + c, wt + 2)

    for head in order:
        for a in range(4):
            load(head, a).start()
        qload(head).start()

    def clear(s, r):
        @pl.loop(0, GROUP)
        def _(i):
            kv[i, s, r] = jnp.zeros((4, TILE, HD), jnp.bfloat16)

    @pl.when(jnp.logical_not(has_left))
    def _():
        for r in range(4):
            clear(0, r)

    @pl.when(jnp.logical_not(has_right))
    def _():
        for r in range(4):
            clear(2, r)

    @pl.when(jnp.logical_not(has_up))
    def _():
        for s in range(3):
            clear(s, 0)

    @pl.when(jnp.logical_not(has_down))
    def _():
        for s in range(3):
            clear(s, 3)

    for t in range(2):
        rows = row_bias(chip, chips, t)
        q_col = iota((TILE, KEYS), 0) % COLS
        k_col = iota((TILE, KEYS), 1) % COLS
        for s in range(3):
            delta = k_col - q_col + (s - 1) * 2 * COLS
            inside = (strip + s - 1 >= 0) & (strip + s - 1 < strips)
            ok = rows & (delta >= -HALF) & (delta < HALF)
            own_bias[t, s] = jnp.where(ok & inside, 0.0, MASKED)
        for n in range(2):
            at = strip + n - half
            far_bias[t, n] = jnp.where(rows & (at >= 0) & (at < strips), 0.0, MASKED)

    def loaded(i):
        for head in (i, GROUP + i):
            for a in range(4):
                load(head, a).wait()
            qload(head).wait()

    greeted = 3 + 2 * (
        has_up.astype(jnp.int32) + has_down.astype(jnp.int32) + has_left.astype(jnp.int32) + has_right.astype(jnp.int32)
    )
    pl.semaphore_wait(barrier, greeted)

    sends_z = jnp.where(core == 1, chip < chips - 1, chip > 0)
    z_chip = jnp.where(core == 1, jnp.minimum(chip + 1, chips - 1), jnp.maximum(chip - 1, 0))
    z_slot = 3 * other

    def z_copy(i, c):
        return remote(
            src.at[c * GROUP + i], kv.at[i, 1, z_slot], z_send.at[i, c], kv_recv.at[i, 1, z_slot], 2 * z_chip + c, wt
        )

    def sib_copy(i):
        return remote(
            src.at[other * GROUP + i], kv.at[i, 1, 1 + core], sib_send.at[i], kv_recv.at[i, 1, 1 + core],
            2 * chip + other, wt,
        )

    def own_copy(i):
        return pltpu.make_async_copy(src.at[core * GROUP + i], kv.at[i, 1, 1 + core], local_sem.at[i])

    sides = ((has_left, -2, 2), (has_right, 2, 0))

    def y_copy(i, d, c):
        _, step, s = sides[d]
        return remote(
            src.at[c * GROUP + i], kv.at[i, s, 1 + core], y_send.at[i, d, c], kv_recv.at[i, s, 1 + core],
            2 * chip + c, wt + step,
        )

    def relay_copy(i, d, n):
        _, step, s = sides[d]
        return remote(
            kv.at[i, 1, 3 * n], kv.at[i, s, 3 * n], relay_send.at[i, d, n], kv_recv.at[i, s, 3 * n], ht, wt + step
        )

    def q_copy(i, c):
        return remote(
            qsrc.at[c * GROUP + i], qb.at[i, 1, core], q_send.at[i, c], q_recv.at[i, 1, core], 2 * chip + c, far
        )

    def qsib_copy(i):
        return remote(
            qsrc.at[other * GROUP + i], qb.at[i, 0, core], qsib_send.at[i], q_recv.at[i, 0, core],
            2 * chip + other, wt,
        )

    def qown_copy(i):
        return pltpu.make_async_copy(qsrc.at[core * GROUP + i], qb.at[i, 0, core], qlocal_sem.at[i])

    def kv_arrived(i, s, r):
        pltpu.make_async_copy(src.at[0], kv.at[i, s, r], kv_recv.at[i, s, r]).wait()

    def send_z(i):
        @pl.when(sends_z)
        def _():
            for c in range(2):
                z_copy(i, c).start()

    def send_q(i):
        for c in range(2):
            q_copy(i, c).start()

    def send_y(i):
        for d in range(2):
            @pl.when(sides[d][0])
            def _():
                for c in range(2):
                    y_copy(i, d, c).start()

    def send_here(i):
        sib_copy(i).start()
        own_copy(i).start()
        qsib_copy(i).start()
        qown_copy(i).start()

    loaded(0)
    send_z(0)
    send_y(0)
    send_q(0)
    loaded(1)
    send_z(1)
    send_here(0)
    loaded(2)
    send_z(2)
    send_q(1)
    loaded(3)
    send_z(3)
    send_q(2)
    send_q(3)
    for i in range(1, GROUP):
        send_here(i)

    ends = (has_up, has_down)

    for i in range(GROUP):
        if i > 0:
            send_y(i)
        for n in range(2):
            @pl.when(ends[n])
            def _():
                kv_arrived(i, 1, 3 * n)
                for d in range(2):
                    @pl.when(sides[d][0])
                    def _():
                        relay_copy(i, d, n).start()

    eye = iota((TILE, TILE), 0) == iota((TILE, TILE), 1)

    def attend(q, i, t, blocks):
        scores = []
        for s, bias in blocks:
            for f in range(2):
                k = kv[i, s, pl.ds(t, 3), f].reshape(KEYS, HD)
                dots = lax.dot_general(q, k, (((1,), (1,)), ((), ())), preferred_element_type=jnp.float32)
                scores.append(dots * (HD**-0.5 * LOG2E) + bias[...])
        top = functools.reduce(jnp.maximum, scores)
        top = jnp.max(top, axis=1, keepdims=True)
        total = jnp.zeros((TILE, KEYS), jnp.float32)
        acc = jnp.zeros((TILE, HD), jnp.float32)
        n = 0
        for s, _ in blocks:
            for f in range(2):
                weights = jnp.exp2(scores[n] - top)
                total = total + weights
                v = kv[i, s, pl.ds(t, 3), 2 + f].reshape(KEYS, HD)
                acc = acc + jnp.dot(weights.astype(jnp.bfloat16), v, preferred_element_type=jnp.float32)
                n += 1
        total = jnp.sum(total, axis=1, keepdims=True)
        return acc * (1.0 / total), top + jnp.log2(total)

    def taps(i):
        lanes = pl.ds(pl.multiple_of((core * GROUP + i) * HD, HD), HD)
        return [[cw_ref[a, pl.ds(b, 1), lanes] for b in range(3)] for a in range(3)], cb_ref[:, lanes]

    def edges(i, t):
        weight, _ = taps(i)
        pick = iota((3 * ROWS, KEYS), 0)
        key = iota((3 * ROWS, KEYS), 1)
        wanted = (ROWS - 1 + pick % ROWS + pick // ROWS) * COLS
        parts = []
        for n, col, b in ((0, COLS - 1, 0), (1, 0, 2)):
            v = kv[i, 1 - half + n, pl.ds(t, 3), 3].reshape(KEYS, HD)
            chosen = jnp.where(key == wanted + col, 1.0, 0.0).astype(jnp.bfloat16)
            picked = jnp.dot(chosen, v, preferred_element_type=jnp.float32)
            parts.append(sum(picked[a * ROWS : (a + 1) * ROWS] * weight[a][b] for a in range(3)))
        return jnp.concatenate(parts, axis=0).astype(jnp.bfloat16)

    def conv(i, t):
        weight, bias = taps(i)
        v = kv[i, 1, pl.ds(t, 3), 3].reshape(KEYS, HD).astype(jnp.float32)
        rows = [v[TILE + (a - 1) * COLS : 2 * TILE + (a - 1) * COLS] for a in range(3)]
        left, here, right = (sum(rows[a] * weight[a][b] for a in range(3)) for b in range(3))
        col = iota((TILE, HD), 0) % COLS
        left = jnp.where(col == 0, 0.0, pltpu.roll(left, 1, 0))
        right = jnp.where(col == COLS - 1, 0.0, pltpu.roll(right, TILE - 1, 0))
        return here + left + right + bias

    def o_copy(i, t):
        return remote(
            far_send.at[i, t], far_recv.at[core, i], o_send.at[i, t], o_recv.at[core, i], 2 * chip + t, far
        )

    def s_copy(i, t):
        return remote(
            stat_send.at[i, t], stat_recv.at[core, i], s_send.at[i, t], s_recv.at[core, i], 2 * chip + t, far
        )

    def own_part_copy(i):
        return remote(own.at[i, other], sib_in.at[i], own_send.at[i], own_recv.at[i], 2 * chip + other, wt)

    def wait_inputs(i):
        own_copy(i).wait()
        qown_copy(i).wait()
        kv_arrived(i, 1, 1 + other)
        pltpu.make_async_copy(qsrc.at[0], qb.at[i, 0, other], q_recv.at[i, 0, other]).wait()
        for t in range(2):
            pltpu.make_async_copy(qsrc.at[0], qb.at[i, 1, t], q_recv.at[i, 1, t]).wait()
        for valid, s in ((has_left, 0), (has_right, 2)):
            @pl.when(valid)
            def _():
                kv_arrived(i, s, 1)
                kv_arrived(i, s, 2)

                @pl.when(has_up)
                def _():
                    kv_arrived(i, s, 0)

                @pl.when(has_down)
                def _():
                    kv_arrived(i, s, 3)

    @pl.loop(0, GROUP)
    def _(i):
        wait_inputs(i)

        @pl.loop(0, 2)
        def _(t):
            o, s = attend(qb[i, 1, t], i, t, [(1 - half + n, far_bias.at[t, n]) for n in range(2)])
            far_send[i, t, :TILE] = o.astype(jnp.bfloat16)
            far_send[i, t, TILE:] = edges(i, t)
            stat_send[i, t] = jnp.sum(jnp.where(eye, s, 0.0), axis=0, keepdims=True)
            s_copy(i, t).start()
            o_copy(i, t).start()

        @pl.loop(0, 2)
        def _(t):
            o, s = attend(qb[i, 0, t], i, t, [(n, own_bias.at[t, n]) for n in range(3)])
            own[i, t, 0] = o
            own[i, t, 1] = conv(i, t)
            own[i, t, 2] = jnp.broadcast_to(s, (TILE, HD))

        own_part_copy(i).start()

    def complete(i, g, mine):
        pltpu.make_async_copy(stat_send.at[i, 0], stat_recv.at[g, i], s_recv.at[g, i]).wait()
        far_s = jnp.sum(jnp.where(eye, stat_recv[g, i], 0.0), axis=1, keepdims=True)
        shift = far_s - mine[2]
        own_w = 1.0 / (1.0 + jnp.exp2(shift))
        far_w = 1.0 / (1.0 + jnp.exp2(-shift))
        here = mine[0] * own_w + mine[1]
        place = iota((TILE, EDGE), 0)
        edge = iota((TILE, EDGE), 1)
        spot = (edge % ROWS) * COLS + (edge // ROWS) * (COLS - 1)
        spread = jnp.where(place == spot, 1.0, 0.0).astype(jnp.bfloat16)
        pltpu.make_async_copy(far_send.at[i, 0], far_recv.at[g, i], o_recv.at[g, i]).wait()
        edge_part = jnp.dot(spread, far_recv[g, i, TILE:], preferred_element_type=jnp.float32)
        there = far_recv[g, i, :TILE].astype(jnp.float32) * far_w
        lanes = pl.ds(pl.multiple_of((g * GROUP + i) * HD, HD), HD)
        out_ref[:, lanes] = (here + there + edge_part).astype(jnp.bfloat16)

    @pl.loop(0, GROUP)
    def _(i):
        pltpu.make_async_copy(own.at[i, 0], sib_in.at[i], own_recv.at[i]).wait()
        complete(i, core, own.at[i, core])
        complete(i, other, sib_in.at[i])

    for i in range(GROUP):
        @pl.when(sends_z)
        def _():
            for c in range(2):
                z_copy(i, c).wait_send()

        sib_copy(i).wait_send()
        qsib_copy(i).wait_send()
        for c in range(2):
            q_copy(i, c).wait_send()
        for d in range(2):
            @pl.when(sides[d][0])
            def _():
                for c in range(2):
                    y_copy(i, d, c).wait_send()
                for n in range(2):
                    @pl.when(ends[n])
                    def _():
                        relay_copy(i, d, n).wait_send()

        for t in range(2):
            o_copy(i, t).wait_send()
            s_copy(i, t).wait_send()
        own_part_copy(i).wait_send()


def shards(chips, strips, queries, keys_new, values_new, keys_cache, values_cache, conv_weight, conv_bias):
    rows, cols, channels = queries.shape
    flat = [x.reshape(TILE, channels) for x in (queries, keys_cache, keys_new, values_cache, values_new)]
    any_spec = pl.BlockSpec(memory_space=pl.ANY)
    vmem_spec = pl.BlockSpec(memory_space=pltpu.VMEM)
    bf16, f32 = jnp.bfloat16, jnp.float32
    dma = pltpu.SemaphoreType.DMA
    out = pl.pallas_call(
        functools.partial(kernel, chips, strips),
        out_shape=pltpu.VMEM((TILE, channels), bf16),
        in_specs=[any_spec] * 5 + [vmem_spec] * 2,
        out_specs=vmem_spec,
        scratch_shapes=[
            pltpu.VMEM((HEADS, 4, TILE, HD), bf16),
            pltpu.VMEM((HEADS, TILE, HD), bf16),
            pltpu.VMEM((GROUP, 3, 4, 4, TILE, HD), bf16),
            pltpu.VMEM((GROUP, 2, 2, TILE, HD), bf16),
            pltpu.VMEM((2, 3, TILE, KEYS), f32),
            pltpu.VMEM((2, 2, TILE, KEYS), f32),
            pltpu.VMEM((GROUP, 2, 3, TILE, HD), f32),
            pltpu.VMEM((GROUP, 3, TILE, HD), f32),
            pltpu.VMEM((GROUP, 2, TILE + EDGE, HD), bf16),
            pltpu.VMEM((2, GROUP, TILE + EDGE, HD), bf16),
            pltpu.VMEM((GROUP, 2, 1, HD), f32),
            pltpu.VMEM((2, GROUP, 1, HD), f32),
            dma((HEADS, 4)), dma((HEADS,)), dma((GROUP,)), dma((GROUP,)),
            dma((GROUP, 2)), dma((GROUP, 2, 2)), dma((GROUP,)), dma((GROUP, 2, 2)), dma((GROUP, 2)), dma((GROUP,)),
            dma((GROUP, 2)), dma((GROUP, 2)), dma((GROUP,)),
            dma((GROUP, 3, 4)), dma((GROUP, 2, 2)), dma((2, GROUP)), dma((2, GROUP)), dma((GROUP,)),
        ],
        compiler_params=pltpu.CompilerParams(
            collective_id=0, has_side_effects=True, vmem_limit_bytes=56 << 20
        ),
    )(*flat, conv_weight, conv_bias.reshape(1, channels))
    return out.reshape(rows, cols, channels)


def solution(mesh):
    placed = (
        P("ht", "wt", None),
        P("ht", "wt", None),
        P("ht", "wt", None),
        P(None, "ht", "wt", None),
        P(None, "ht", "wt", None),
        P(),
        P(),
    )
    body = functools.partial(shards, mesh.shape["ht"] // 2, mesh.shape["wt"] // 2)
    return jax.shard_map(body, mesh=mesh, in_specs=placed, out_specs=P("ht", "wt", None), check_vma=False)
```

```python
import functools

import jax
import jax.numpy as jnp
from jax import lax
from jax.experimental import pallas as pl
from jax.experimental.pallas import tpu as pltpu
from jax.sharding import PartitionSpec as P

MESH = pl.DeviceIdType.MESH
HD = 128
WIN = 32
HALF = WIN // 2
ROWS = 16
COLS = 8
TILE = ROWS * COLS
HEADS = 8
GROUP = HEADS // 2
KEYS = 3 * TILE
EDGE = 2 * ROWS
LOG2E = 1.4426950408889634
MASKED = -1e30


def iota(shape, dim):
    return lax.broadcasted_iota(jnp.int32, shape, dim)


def row_bias(chip, chips, t):
    q_row = iota((TILE, KEYS), 0) // COLS
    k_row = iota((TILE, KEYS), 1) // COLS - ROWS
    frame_row = k_row + (2 * chip + t) * ROWS
    delta = k_row - q_row
    return (delta >= -HALF) & (delta < HALF) & (frame_row >= 0) & (frame_row < chips * 2 * ROWS)


def kernel(
    chips, strips, q_ref, kc_ref, kn_ref, vc_ref, vn_ref, cw_ref, cb_ref, out_ref,
    src, qsrc, kv, qb, own_bias, far_bias, own, sib_in, far_send, far_recv, stat_send, stat_recv,
    load_sem, qload_sem, local_sem, qlocal_sem,
    z_send, y_send, sib_send, relay_send, q_send, qsib_send, o_send, s_send, own_send,
    kv_recv, q_recv, o_recv, s_recv, own_recv,
):
    ht = lax.axis_index("ht")
    wt = lax.axis_index("wt")
    chip, core = ht // 2, ht % 2
    strip, half = wt // 2, wt % 2
    other = 1 - core
    far = wt + 1 - 2 * half
    has_up, has_down = chip > 0, chip < chips - 1
    has_left, has_right = strip > 0, strip < strips - 1

    def remote(source, target, send_sem, recv_sem, to_ht, to_wt):
        return pltpu.make_async_remote_copy(
            src_ref=source, dst_ref=target, send_sem=send_sem, recv_sem=recv_sem,
            device_id={"ht": to_ht, "wt": to_wt}, device_id_type=MESH,
        )

    inputs = (kc_ref, kn_ref, vc_ref, vn_ref)
    order = [g * GROUP + i for i in range(GROUP) for g in range(2)]

    def load(head, a):
        lanes = pl.ds(head * HD, HD)
        return pltpu.make_async_copy(inputs[a].at[:, lanes], src.at[head, a], load_sem.at[head, a])

    def qload(head):
        return pltpu.make_async_copy(q_ref.at[:, pl.ds(head * HD, HD)], qsrc.at[head], qload_sem.at[head])

    barrier = pltpu.get_barrier_semaphore()

    def greet(to_ht, to_wt):
        pl.semaphore_signal(barrier, inc=1, device_id={"ht": to_ht, "wt": to_wt}, device_id_type=MESH)

    for c in range(2):
        greet(2 * chip + c, far)
    greet(2 * chip + other, wt)
    for c in range(2):
        @pl.when(has_up)
        def _():
            greet(2 * (chip - 1) + c, wt)

        @pl.when(has_down)
        def _():
            greet(2 * (chip + 1) + c, wt)

        @pl.when(has_left)
        def _():
            greet(2 * chip + c, wt - 2)

        @pl.when(has_right)
        def _():
            greet(2 * chip + c, wt + 2)

    for head in order:
        for a in range(4):
            load(head, a).start()
        qload(head).start()

    def clear(s, r):
        @pl.loop(0, GROUP)
        def _(i):
            kv[i, s, r] = jnp.zeros((4, TILE, HD), jnp.bfloat16)

    @pl.when(jnp.logical_not(has_left))
    def _():
        for r in range(4):
            clear(0, r)

    @pl.when(jnp.logical_not(has_right))
    def _():
        for r in range(4):
            clear(2, r)

    @pl.when(jnp.logical_not(has_up))
    def _():
        for s in range(3):
            clear(s, 0)

    @pl.when(jnp.logical_not(has_down))
    def _():
        for s in range(3):
            clear(s, 3)

    for t in range(2):
        rows = row_bias(chip, chips, t)
        q_col = iota((TILE, KEYS), 0) % COLS
        k_col = iota((TILE, KEYS), 1) % COLS
        for s in range(3):
            delta = k_col - q_col + (s - 1) * 2 * COLS
            inside = (strip + s - 1 >= 0) & (strip + s - 1 < strips)
            ok = rows & (delta >= -HALF) & (delta < HALF)
            own_bias[t, s] = jnp.where(ok & inside, 0.0, MASKED)
        for n in range(2):
            at = strip + n - half
            far_bias[t, n] = jnp.where(rows & (at >= 0) & (at < strips), 0.0, MASKED)

    def loaded(i):
        for head in (i, GROUP + i):
            for a in range(4):
                load(head, a).wait()
            qload(head).wait()

    greeted = 3 + 2 * (
        has_up.astype(jnp.int32) + has_down.astype(jnp.int32) + has_left.astype(jnp.int32) + has_right.astype(jnp.int32)
    )
    pl.semaphore_wait(barrier, greeted)

    sends_z = jnp.where(core == 1, chip < chips - 1, chip > 0)
    z_chip = jnp.where(core == 1, jnp.minimum(chip + 1, chips - 1), jnp.maximum(chip - 1, 0))
    z_slot = 3 * other

    def z_copy(i, c):
        return remote(
            src.at[c * GROUP + i], kv.at[i, 1, z_slot], z_send.at[i, c], kv_recv.at[i, 1, z_slot], 2 * z_chip + c, wt
        )

    def sib_copy(i):
        return remote(
            src.at[other * GROUP + i], kv.at[i, 1, 1 + core], sib_send.at[i], kv_recv.at[i, 1, 1 + core],
            2 * chip + other, wt,
        )

    def own_copy(i):
        return pltpu.make_async_copy(src.at[core * GROUP + i], kv.at[i, 1, 1 + core], local_sem.at[i])

    sides = ((has_left, -2, 2), (has_right, 2, 0))

    def y_copy(i, d, c):
        _, step, s = sides[d]
        return remote(
            src.at[c * GROUP + i], kv.at[i, s, 1 + core], y_send.at[i, d, c], kv_recv.at[i, s, 1 + core],
            2 * chip + c, wt + step,
        )

    def relay_copy(i, d, n):
        _, step, s = sides[d]
        return remote(
            kv.at[i, 1, 3 * n], kv.at[i, s, 3 * n], relay_send.at[i, d, n], kv_recv.at[i, s, 3 * n], ht, wt + step
        )

    def q_copy(i, c):
        return remote(
            qsrc.at[c * GROUP + i], qb.at[i, 1, core], q_send.at[i, c], q_recv.at[i, 1, core], 2 * chip + c, far
        )

    def qsib_copy(i):
        return remote(
            qsrc.at[other * GROUP + i], qb.at[i, 0, core], qsib_send.at[i], q_recv.at[i, 0, core],
            2 * chip + other, wt,
        )

    def qown_copy(i):
        return pltpu.make_async_copy(qsrc.at[core * GROUP + i], qb.at[i, 0, core], qlocal_sem.at[i])

    def kv_arrived(i, s, r):
        pltpu.make_async_copy(src.at[0], kv.at[i, s, r], kv_recv.at[i, s, r]).wait()

    def send_z(i):
        @pl.when(sends_z)
        def _():
            for c in range(2):
                z_copy(i, c).start()

    def send_q(i):
        q_copy(i, core).start()
        q_copy(i, other).start()

    def send_y(i):
        for d in range(2):
            @pl.when(sides[d][0])
            def _():
                for c in range(2):
                    y_copy(i, d, c).start()

    def send_here(i):
        sib_copy(i).start()
        own_copy(i).start()
        qsib_copy(i).start()
        qown_copy(i).start()

    loaded(0)
    send_z(0)
    send_y(0)
    send_q(0)
    loaded(1)
    send_z(1)
    send_here(0)
    loaded(2)
    send_z(2)
    send_q(1)
    loaded(3)
    send_z(3)
    send_q(2)
    send_q(3)
    for i in range(1, GROUP):
        send_here(i)

    ends = (has_up, has_down)

    for i in range(GROUP):
        if i > 0:
            send_y(i)
        for n in range(2):
            @pl.when(ends[n])
            def _():
                kv_arrived(i, 1, 3 * n)
                for d in range(2):
                    @pl.when(sides[d][0])
                    def _():
                        relay_copy(i, d, n).start()

    eye = iota((TILE, TILE), 0) == iota((TILE, TILE), 1)

    def attend(q, i, t, blocks):
        scores = []
        for s, bias in blocks:
            for f in range(2):
                k = kv[i, s, pl.ds(t, 3), f].reshape(KEYS, HD)
                dots = lax.dot_general(q, k, (((1,), (1,)), ((), ())), preferred_element_type=jnp.float32)
                scores.append(dots * (HD**-0.5 * LOG2E) + bias[...])
        top = functools.reduce(jnp.maximum, scores)
        top = jnp.max(top, axis=1, keepdims=True)
        total = jnp.zeros((TILE, KEYS), jnp.float32)
        acc = jnp.zeros((TILE, HD), jnp.float32)
        n = 0
        for s, _ in blocks:
            for f in range(2):
                weights = jnp.exp2(scores[n] - top)
                total = total + weights
                v = kv[i, s, pl.ds(t, 3), 2 + f].reshape(KEYS, HD)
                acc = acc + jnp.dot(weights.astype(jnp.bfloat16), v, preferred_element_type=jnp.float32)
                n += 1
        total = jnp.sum(total, axis=1, keepdims=True)
        return acc * (1.0 / total), top + jnp.log2(total)

    def taps(i):
        lanes = pl.ds(pl.multiple_of((core * GROUP + i) * HD, HD), HD)
        return [[cw_ref[a, pl.ds(b, 1), lanes] for b in range(3)] for a in range(3)], cb_ref[:, lanes]

    def edges(i, t):
        weight, _ = taps(i)
        pick = iota((3 * ROWS, KEYS), 0)
        key = iota((3 * ROWS, KEYS), 1)
        wanted = (ROWS - 1 + pick % ROWS + pick // ROWS) * COLS
        parts = []
        for n, col, b in ((0, COLS - 1, 0), (1, 0, 2)):
            v = kv[i, 1 - half + n, pl.ds(t, 3), 3].reshape(KEYS, HD)
            chosen = jnp.where(key == wanted + col, 1.0, 0.0).astype(jnp.bfloat16)
            picked = jnp.dot(chosen, v, preferred_element_type=jnp.float32)
            parts.append(sum(picked[a * ROWS : (a + 1) * ROWS] * weight[a][b] for a in range(3)))
        return jnp.concatenate(parts, axis=0).astype(jnp.bfloat16)

    def conv(i, t):
        weight, bias = taps(i)
        v = kv[i, 1, pl.ds(t, 3), 3].reshape(KEYS, HD).astype(jnp.float32)
        rows = [v[TILE + (a - 1) * COLS : 2 * TILE + (a - 1) * COLS] for a in range(3)]
        left, here, right = (sum(rows[a] * weight[a][b] for a in range(3)) for b in range(3))
        col = iota((TILE, HD), 0) % COLS
        left = jnp.where(col == 0, 0.0, pltpu.roll(left, 1, 0))
        right = jnp.where(col == COLS - 1, 0.0, pltpu.roll(right, TILE - 1, 0))
        return here + left + right + bias

    def o_copy(i, t):
        return remote(
            far_send.at[i, t], far_recv.at[core, i], o_send.at[i, t], o_recv.at[core, i], 2 * chip + t, far
        )

    def s_copy(i, t):
        return remote(
            stat_send.at[i, t], stat_recv.at[core, i], s_send.at[i, t], s_recv.at[core, i], 2 * chip + t, far
        )

    def own_part_copy(i):
        return remote(own.at[i, other], sib_in.at[i], own_send.at[i], own_recv.at[i], 2 * chip + other, wt)

    def wait_inputs(i):
        own_copy(i).wait()
        qown_copy(i).wait()
        kv_arrived(i, 1, 1 + other)
        pltpu.make_async_copy(qsrc.at[0], qb.at[i, 0, other], q_recv.at[i, 0, other]).wait()
        for t in range(2):
            pltpu.make_async_copy(qsrc.at[0], qb.at[i, 1, t], q_recv.at[i, 1, t]).wait()
        for valid, s in ((has_left, 0), (has_right, 2)):
            @pl.when(valid)
            def _():
                kv_arrived(i, s, 1)
                kv_arrived(i, s, 2)

                @pl.when(has_up)
                def _():
                    kv_arrived(i, s, 0)

                @pl.when(has_down)
                def _():
                    kv_arrived(i, s, 3)

    @pl.loop(0, GROUP)
    def _(i):
        wait_inputs(i)

        @pl.loop(0, 2)
        def _(t):
            o, s = attend(qb[i, 1, t], i, t, [(1 - half + n, far_bias.at[t, n]) for n in range(2)])
            far_send[i, t, :TILE] = o.astype(jnp.bfloat16)
            far_send[i, t, TILE:] = edges(i, t)
            stat_send[i, t] = jnp.sum(jnp.where(eye, s, 0.0), axis=0, keepdims=True)
            s_copy(i, t).start()
            o_copy(i, t).start()

        @pl.loop(0, 2)
        def _(t):
            o, s = attend(qb[i, 0, t], i, t, [(n, own_bias.at[t, n]) for n in range(3)])
            own[i, t, 0] = o
            own[i, t, 1] = conv(i, t)
            own[i, t, 2] = jnp.broadcast_to(s, (TILE, HD))

        own_part_copy(i).start()

    def complete(i, g, mine):
        pltpu.make_async_copy(stat_send.at[i, 0], stat_recv.at[g, i], s_recv.at[g, i]).wait()
        far_s = jnp.sum(jnp.where(eye, stat_recv[g, i], 0.0), axis=1, keepdims=True)
        shift = far_s - mine[2]
        own_w = 1.0 / (1.0 + jnp.exp2(shift))
        far_w = 1.0 / (1.0 + jnp.exp2(-shift))
        here = mine[0] * own_w + mine[1]
        place = iota((TILE, EDGE), 0)
        edge = iota((TILE, EDGE), 1)
        spot = (edge % ROWS) * COLS + (edge // ROWS) * (COLS - 1)
        spread = jnp.where(place == spot, 1.0, 0.0).astype(jnp.bfloat16)
        pltpu.make_async_copy(far_send.at[i, 0], far_recv.at[g, i], o_recv.at[g, i]).wait()
        edge_part = jnp.dot(spread, far_recv[g, i, TILE:], preferred_element_type=jnp.float32)
        there = far_recv[g, i, :TILE].astype(jnp.float32) * far_w
        lanes = pl.ds(pl.multiple_of((g * GROUP + i) * HD, HD), HD)
        out_ref[:, lanes] = (here + there + edge_part).astype(jnp.bfloat16)

    @pl.loop(0, GROUP)
    def _(i):
        pltpu.make_async_copy(own.at[i, 0], sib_in.at[i], own_recv.at[i]).wait()
        complete(i, core, own.at[i, core])
        complete(i, other, sib_in.at[i])

    for i in range(GROUP):
        @pl.when(sends_z)
        def _():
            for c in range(2):
                z_copy(i, c).wait_send()

        sib_copy(i).wait_send()
        qsib_copy(i).wait_send()
        for c in range(2):
            q_copy(i, c).wait_send()
        for d in range(2):
            @pl.when(sides[d][0])
            def _():
                for c in range(2):
                    y_copy(i, d, c).wait_send()
                for n in range(2):
                    @pl.when(ends[n])
                    def _():
                        relay_copy(i, d, n).wait_send()

        for t in range(2):
            o_copy(i, t).wait_send()
            s_copy(i, t).wait_send()
        own_part_copy(i).wait_send()


def shards(chips, strips, queries, keys_new, values_new, keys_cache, values_cache, conv_weight, conv_bias):
    rows, cols, channels = queries.shape
    flat = [x.reshape(TILE, channels) for x in (queries, keys_cache, keys_new, values_cache, values_new)]
    any_spec = pl.BlockSpec(memory_space=pl.ANY)
    vmem_spec = pl.BlockSpec(memory_space=pltpu.VMEM)
    bf16, f32 = jnp.bfloat16, jnp.float32
    dma = pltpu.SemaphoreType.DMA
    out = pl.pallas_call(
        functools.partial(kernel, chips, strips),
        out_shape=pltpu.VMEM((TILE, channels), bf16),
        in_specs=[any_spec] * 5 + [vmem_spec] * 2,
        out_specs=vmem_spec,
        scratch_shapes=[
            pltpu.VMEM((HEADS, 4, TILE, HD), bf16),
            pltpu.VMEM((HEADS, TILE, HD), bf16),
            pltpu.VMEM((GROUP, 3, 4, 4, TILE, HD), bf16),
            pltpu.VMEM((GROUP, 2, 2, TILE, HD), bf16),
            pltpu.VMEM((2, 3, TILE, KEYS), f32),
            pltpu.VMEM((2, 2, TILE, KEYS), f32),
            pltpu.VMEM((GROUP, 2, 3, TILE, HD), f32),
            pltpu.VMEM((GROUP, 3, TILE, HD), f32),
            pltpu.VMEM((GROUP, 2, TILE + EDGE, HD), bf16),
            pltpu.VMEM((2, GROUP, TILE + EDGE, HD), bf16),
            pltpu.VMEM((GROUP, 2, 1, HD), f32),
            pltpu.VMEM((2, GROUP, 1, HD), f32),
            dma((HEADS, 4)), dma((HEADS,)), dma((GROUP,)), dma((GROUP,)),
            dma((GROUP, 2)), dma((GROUP, 2, 2)), dma((GROUP,)), dma((GROUP, 2, 2)), dma((GROUP, 2)), dma((GROUP,)),
            dma((GROUP, 2)), dma((GROUP, 2)), dma((GROUP,)),
            dma((GROUP, 3, 4)), dma((GROUP, 2, 2)), dma((2, GROUP)), dma((2, GROUP)), dma((GROUP,)),
        ],
        compiler_params=pltpu.CompilerParams(
            collective_id=0, has_side_effects=True, vmem_limit_bytes=56 << 20
        ),
    )(*flat, conv_weight, conv_bias.reshape(1, channels))
    return out.reshape(rows, cols, channels)


def solution(mesh):
    placed = (
        P("ht", "wt", None),
        P("ht", "wt", None),
        P("ht", "wt", None),
        P(None, "ht", "wt", None),
        P(None, "ht", "wt", None),
        P(),
        P(),
    )
    body = functools.partial(shards, mesh.shape["ht"] // 2, mesh.shape["wt"] // 2)
    return jax.shard_map(body, mesh=mesh, in_specs=placed, out_specs=P("ht", "wt", None), check_vma=False)
```
